32 devices in a mesh: grp: 2 (over x), vir: 16 (over z, y, core).
Axes of the slice: x: 2, y: 2, z: 4, core: 2. Of those that a mesh axis runs over, the one named last changes fastest.
Arguments:
- amplitudes: bfloat16 [256, 1024, 1024], P(('grp', 'vir')), parts along dimension 0, may hold values from -0.0625 to 0.0625
- integrals: bfloat16 [2, 128, 1024, 1024], P('grp', None, 'vir'), parts along dimension 0, may hold values from -6 to 6
- pair_energy: float32 [2], P('grp'), parts along dimension 0, may hold values from -3 to -0.5
- vir_energy: float32 [2048], P('grp'), parts along dimension 0, may hold values from 0.25 to 3
Outputs:
- update: float32 [2048, 1, 1024], P(('grp', 'vir')), parts along dimension 0
The draws below stay inside these ranges and needn't reach their ends.
There are 2 independent parts, one for each index of `grp`. The reference program is written for one: setup_inputs(seed, part) draws one part's arguments, and reference() takes and returns one part's arrays. A program takes and returns all parts, laid end to end along the dimension named above; each array names one. Nothing has to cross between parts.
All inputs are finite; a program needn't handle non-finite values.
Results may differ from the reference program's by a relative error of at most 0.0003.
Values may be sent and summed in bfloat16 or wider, within the bound.
No kernel may reach another device: no remote copies, remote signals or barrier semaphores. Data moves between devices by JAX's collectives and lax.ppermute only.
A program may use at most 128 MiB of HBM per device.

```python
import jax
import jax.numpy as jnp
from jax import lax

O = 128
V = 1024
J = 1


def shard_levels(stream_key, extent, cuts, least, high):
    level = 1.0
    for axis_at, shards_of in cuts:
        heights = jax.random.uniform(jax.random.fold_in(jax.random.fold_in(stream_key, 6), axis_at), (shards_of,), jnp.float32, least / len(cuts), high / len(cuts))
        level = level * jnp.repeat(jnp.exp(heights), extent[axis_at] // shards_of).reshape((-1,) + (1,) * (len(extent) - 1 - axis_at))
    return level


def noise(stream_key, extent, deviation, limit, pieces=(), kind=jnp.bfloat16):
    result = deviation * jax.random.normal(stream_key, extent, jnp.float32)
    if pieces:
        result = result * shard_levels(stream_key, extent, pieces, -0.22, 0.18)
    return jnp.clip(result, -limit, limit).astype(kind)


def setup_inputs(seed: int = 0, part: int = 0) -> dict:
    keys = jax.random.split(jax.random.key(seed), 5)
    part_keys = jax.random.split(jax.random.fold_in(keys[4], part), 5)
    return {
        "amplitudes": noise(part_keys[0], (O, V, V), (O * V // 16) ** -0.5, 0.0625, ((0, 16),)),
        "integrals": noise(part_keys[1], (J, O, V, V), 1.0, 6.0, ((2, 16),)),
        "pair_energy": jnp.clip(jax.random.uniform(part_keys[2], (J,), jnp.float32, -3.0, -0.5), -3.0, -0.5),
        "vir_energy": jnp.clip(jax.random.uniform(part_keys[3], (V,), jnp.float32, 0.25, 3.0), 0.25, 3.0),
    }


def reference(amplitudes, integrals, pair_energy, vir_energy):
    cyclic_term = jnp.einsum("lgif,gfh->ilh", integrals.astype(jnp.float32), amplitudes.astype(jnp.float32), precision=lax.Precision.HIGHEST)
    paired = cyclic_term + jnp.transpose(cyclic_term, (2, 1, 0))
    energy_denominator = pair_energy[None, :, None] - vir_energy[None, None, :] - vir_energy[:, None, None]
    return paired / energy_denominator
```

```python
import jax
import jax.numpy as jnp
from jax import lax
from jax.sharding import PartitionSpec as P

AXIS = "vir"
IN_FLIGHT = 4


def denominator(pair_energy, vir_energy, start, rows):
    mine = lax.dynamic_slice_in_dim(vir_energy, start, rows, 0)
    return pair_energy[None, :, None] - vir_energy[None, None, :] - mine[:, None, None]


def gathered_body(amplitudes, integrals, pair_energy, vir_energy):
    blocks = lax.all_to_all(integrals, AXIS, split_axis=1, concat_axis=2, tiled=True)
    rows = blocks.shape[2] // lax.axis_size(AXIS)
    part = jnp.einsum("lgif,gfh->ilh", blocks, amplitudes, preferred_element_type=jnp.float32)
    cycle = lax.psum_scatter(part, AXIS, scatter_dimension=0, tiled=True)
    swapped = lax.all_to_all(cycle, AXIS, split_axis=2, concat_axis=0, tiled=True)
    paired = cycle + jnp.transpose(swapped, (2, 1, 0))
    return paired / denominator(pair_energy, vir_energy, lax.axis_index(AXIS) * rows, rows)


def paired_with(n, s):
    return [(i, i ^ s) for i in range(n)]


def after(x, *deps):
    deps = [d for d in deps if d is not None]
    if not deps:
        return x
    return lax.optimization_barrier((x, *deps))[0]


def exchanged_body(amplitudes, integrals, pair_energy, vir_energy):
    n = lax.axis_size(AXIS)
    half = n // 2
    me = lax.axis_index(AXIS)
    own, e, a = amplitudes.shape
    rows = integrals.shape[2]
    source = integrals.reshape(integrals.shape[1:])
    chunks = 4
    r = rows // chunks

    order = []
    for k in range(half):
        order.append(half + k)
        if k + 1 < half:
            order.append(k + 1)

    def piece(s, start, size, *deps):
        src = after(source, *deps)
        return lax.dynamic_slice(src, ((me ^ s) * own, start, 0), (own, size, e))

    flight = []
    sums = None
    stage = None
    cycle_rows = []
    for q in range(chunks):
        got = {0: lax.dynamic_slice(source, (me * own, q * r, 0), (own, r, e))}
        pending = stage or []
        for k, s in enumerate(order):
            deps = [flight[-IN_FLIGHT]] if len(flight) >= IN_FLIGHT else []
            if pending and k % 3 == 2:
                deps.append(pending.pop(0)())
            out = lax.ppermute(piece(s, q * r, r, *deps), AXIS, paired_with(n, s))
            flight.append(out)
            got[s] = out
        while pending:
            pending.pop(0)()
        lhs = jnp.concatenate([got[s] for s in range(n)], axis=1)

        state = {}

        def multiply(lhs=lhs, state=state):
            state["x"] = jnp.einsum(
                "mre,mea->ra", lhs, amplitudes, preferred_element_type=jnp.float32
            ).reshape(n, r, a)
            return state["x"]

        def halve(bit, state=state):
            x = state["x"].reshape(-1, 2, r, a)
            moved = lax.ppermute(x[:, 1], AXIS, paired_with(n, bit))
            state["x"] = x[:, 0] + moved
            return state["x"]

        def last(state=state):
            x = state["x"]
            moved = lax.ppermute(x[1], AXIS, paired_with(n, half))
            state["x"] = x[0] + moved
            cycle_rows.append(state["x"])
            return state["x"]

        stage = [multiply]
        bit = 1
        while bit < half:
            stage.append(lambda bit=bit, halve=halve: halve(bit))
            bit *= 2
        stage.append(last)
    for step in stage:
        step()
    cycle = jnp.concatenate(cycle_rows, axis=0)
    swapped = lax.all_to_all(
        cycle.reshape(rows, n, a // n).transpose(1, 0, 2), AXIS, split_axis=0, concat_axis=0, tiled=True
    )
    paired = cycle + swapped.reshape(n * rows, a // n).T
    return paired[:, None, :] / denominator(pair_energy, vir_energy, me * rows, rows)


def solution(mesh):
    n = mesh.shape[AXIS]
    body = exchanged_body if n & (n - 1) == 0 and n <= 16 else gathered_body
    in_specs = (P(("grp", AXIS), None, None), P("grp", None, AXIS, None), P("grp"), P("grp"))
    out_specs = P(("grp", AXIS), None, None)
    return jax.shard_map(body, mesh=mesh, in_specs=in_specs, out_specs=out_specs, check_vma=False)
```

```python
import functools
import jax
import jax.numpy as jnp
from jax import lax
from jax.experimental import pallas as pl
from jax.experimental.pallas import tpu as pltpu
from jax.sharding import PartitionSpec as P

AXIS = "vir"
CHUNKS = (24, 16, 16, 8)


def denominator(pair_energy, vir_energy, start, rows):
    mine = lax.dynamic_slice_in_dim(vir_energy, start, rows, 0)
    return pair_energy[None, :, None] - vir_energy[None, None, :] - mine[:, None, None]


def gathered_body(amplitudes, integrals, pair_energy, vir_energy):
    blocks = lax.all_to_all(integrals, AXIS, split_axis=1, concat_axis=2, tiled=True)
    rows = blocks.shape[2] // lax.axis_size(AXIS)
    part = jnp.einsum("lgif,gfh->ilh", blocks, amplitudes, preferred_element_type=jnp.float32)
    cycle = lax.psum_scatter(part, AXIS, scatter_dimension=0, tiled=True)
    swapped = lax.all_to_all(cycle, AXIS, split_axis=2, concat_axis=0, tiled=True)
    paired = cycle + jnp.transpose(swapped, (2, 1, 0))
    return paired / denominator(pair_energy, vir_energy, lax.axis_index(AXIS) * rows, rows)


def after(x, *deps):
    return lax.optimization_barrier((x, *deps))[0] if deps else x


def product_kernel(lhs, amp, out):
    @pl.when(pl.program_id(0) == 0)
    def _():
        out[...] = jnp.zeros_like(out)

    n, _, r, e = lhs.shape
    rows = lhs[:, 0].astype(jnp.float32).reshape(n * r, e).astype(jnp.bfloat16)
    out[...] += jnp.dot(rows, amp[0], preferred_element_type=jnp.float32)


def product(blocks, amplitudes):
    n, own, r, e = blocks.shape
    a = amplitudes.shape[2]
    return pl.pallas_call(
        product_kernel,
        grid=(own,),
        in_specs=[
            pl.BlockSpec((n, 1, r, e), lambda m: (0, m, 0, 0)),
            pl.BlockSpec((1, e, a), lambda m: (m, 0, 0)),
        ],
        out_specs=pl.BlockSpec((n * r, a), lambda m: (0, 0)),
        out_shape=jax.ShapeDtypeStruct((n * r, a), jnp.float32),
        compiler_params=pltpu.CompilerParams(vmem_limit_bytes=40 * 1024 * 1024),
        cost_estimate=pl.CostEstimate(
            flops=2 * n * r * own * e * a,
            bytes_accessed=2 * own * e * (a + n * r) + 4 * n * r * a,
            transcendentals=0,
        ),
    )(blocks, amplitudes)


def exchanged_body(amplitudes, integrals, pair_energy, vir_energy):
    n = lax.axis_size(AXIS)
    me = lax.axis_index(AXIS)
    own, e, a = amplitudes.shape
    rows = integrals.shape[2]
    source = integrals.reshape(n, own, rows, e)
    width = a // n
    starts = [sum(CHUNKS[:q]) for q in range(len(CHUNKS))]

    def exchange(x):
        return lax.all_to_all(x, AXIS, split_axis=0, concat_axis=0, tiled=True)

    def reduced(part, r):
        blocks = part.reshape(n, r, a)
        bit = 1
        while bit < n:
            odd = (me & bit) != 0
            pair = blocks.reshape(-1, 2, r, a)
            mine = jnp.where(odd, pair[:, 1], pair[:, 0])
            other = jnp.where(odd, pair[:, 0], pair[:, 1])
            blocks = mine + lax.ppermute(other, AXIS, [(i, i ^ bit) for i in range(n)])
            bit *= 2
        return blocks[0]

    received, done = [], []
    for q, r in enumerate(CHUNKS):
        x = source
        if q >= 2:
            x = after(x, received[q - 2])
        x = x[:, :, starts[q] : starts[q] + r]
        if q >= 1:
            x = after(x, received[q - 1], *done[q - 2 : q - 1] if q >= 2 else ())
        received.append(exchange(x))
        if q >= 1:
            part = product(received[q - 1], amplitudes)
            done.append(reduced(part, CHUNKS[q - 1]))
    early = jnp.concatenate(done, axis=0)
    er = early.shape[0]
    early_swap = exchange(after(early.reshape(er, n, width).transpose(1, 0, 2), received[-1]))
    late = CHUNKS[-1]
    part = product(received[-1], amplitudes)
    row_part = part.reshape(n, late, a)
    col_part = part.reshape(n * late, n, width).transpose(1, 0, 2)
    got = exchange(after(jnp.concatenate([row_part, col_part.reshape(n, late, a)], axis=1), early_swap))
    got = got.sum(0)
    late_rows = got[:late]
    late_swap = got[late:].reshape(n, late, width)
    cycle = jnp.concatenate([early, late_rows], axis=0)
    swapped = jnp.concatenate([early_swap, late_swap], axis=1).reshape(n * rows, width)
    paired = cycle + swapped.T
    return paired[:, None, :] / denominator(pair_energy, vir_energy, me * rows, rows)


def solution(mesh):
    n = mesh.shape[AXIS]
    body = exchanged_body if n <= 16 else gathered_body
    in_specs = (P(("grp", AXIS), None, None), P("grp", None, AXIS, None), P("grp"), P("grp"))
    out_specs = P(("grp", AXIS), None, None)
    return jax.shard_map(body, mesh=mesh, in_specs=in_specs, out_specs=out_specs, check_vma=False)
```

```python
import functools
import jax
import jax.numpy as jnp
from jax import lax
from jax.experimental import pallas as pl
from jax.experimental.pallas import tpu as pltpu
from jax.sharding import PartitionSpec as P

AXIS = "vir"
CHUNKS = (8, 32, 16, 8)
STEPS = (2, 1)


def denominator(pair_energy, vir_energy, start, rows):
    mine = lax.dynamic_slice_in_dim(vir_energy, start, rows, 0)
    return pair_energy[None, :, None] - vir_energy[None, None, :] - mine[:, None, None]


def gathered_body(amplitudes, integrals, pair_energy, vir_energy):
    blocks = lax.all_to_all(integrals, AXIS, split_axis=1, concat_axis=2, tiled=True)
    rows = blocks.shape[2] // lax.axis_size(AXIS)
    part = jnp.einsum("lgif,gfh->ilh", blocks, amplitudes, preferred_element_type=jnp.float32)
    cycle = lax.psum_scatter(part, AXIS, scatter_dimension=0, tiled=True)
    swapped = lax.all_to_all(cycle, AXIS, split_axis=2, concat_axis=0, tiled=True)
    paired = cycle + jnp.transpose(swapped, (2, 1, 0))
    return paired / denominator(pair_energy, vir_energy, lax.axis_index(AXIS) * rows, rows)


def after(x, *deps):
    return lax.optimization_barrier((x, *deps))[0] if deps else x


def product_kernel(blocks, amp, out):
    n, owned, r, e = blocks.shape

    def rows_of(m):
        rows = blocks[:, m]
        if r % 16:
            rows = rows.astype(jnp.float32).reshape(n * r, e).astype(jnp.bfloat16)
        return rows.reshape(n * r, e)

    lhs = jnp.concatenate([rows_of(m) for m in range(owned)], axis=1)
    part = jnp.dot(lhs, amp[...].reshape(owned * e, -1), preferred_element_type=jnp.float32)

    @pl.when(pl.program_id(0) == 0)
    def _():
        out[...] = part

    @pl.when(pl.program_id(0) != 0)
    def _():
        out[...] += part


def product(blocks, amplitudes):
    n, own, r, e = blocks.shape
    a = amplitudes.shape[2]
    step = next(s for s in STEPS if own % s == 0)
    return pl.pallas_call(
        product_kernel,
        grid=(own // step,),
        in_specs=[
            pl.BlockSpec((n, step, r, e), lambda m: (0, m, 0, 0)),
            pl.BlockSpec((step, e, a), lambda m: (m, 0, 0)),
        ],
        out_specs=pl.BlockSpec((n * r, a), lambda m: (0, 0)),
        out_shape=jax.ShapeDtypeStruct((n * r, a), jnp.float32),
        compiler_params=pltpu.CompilerParams(vmem_limit_bytes=48 * 1024 * 1024),
        cost_estimate=pl.CostEstimate(
            flops=2 * n * r * own * e * a,
            bytes_accessed=2 * own * e * (a + n * r) + 4 * n * r * a,
            transcendentals=0,
        ),
    )(blocks, amplitudes)


def exchanged_body(amplitudes, integrals, pair_energy, vir_energy):
    n = lax.axis_size(AXIS)
    chips = n // 2
    me = lax.axis_index(AXIS)
    core = me % 2
    own, e, a = amplitudes.shape
    rows = integrals.shape[2]
    source = integrals.reshape(n, own, rows, e)
    width = a // chips
    same_core = [list(range(c, n, 2)) for c in range(2)]
    starts = [sum(CHUNKS[:q]) for q in range(len(CHUNKS))]

    def exchange(x, groups=None):
        return lax.all_to_all(
            x, AXIS, split_axis=0, concat_axis=0, tiled=True, axis_index_groups=groups
        )

    def halve(blocks, bit):
        odd = (me & bit) != 0
        pair = blocks.reshape(-1, 2, *blocks.shape[1:])
        mine = jnp.where(odd, pair[:, 1], pair[:, 0])
        other = jnp.where(odd, pair[:, 0], pair[:, 1])
        return mine + lax.ppermute(other, AXIS, [(i, i ^ bit) for i in range(n)])

    received, near, done = [], [], []
    for q, r in enumerate(CHUNKS):
        x = source
        if q >= 2:
            x = after(x, received[q - 2])
        x = x[:, :, starts[q] : starts[q] + r]
        if q >= 1:
            x = after(x, received[q - 1], *done[q - 2 : q - 1] if q >= 2 else ())
        received.append(exchange(x))
        if q >= 1:
            blocks = product(received[q - 1], amplitudes).reshape(n, CHUNKS[q - 1], a)
            bit = 1
            while 2 * bit < n:
                blocks = halve(blocks, bit)
                bit *= 2
            near.append(blocks)
            done.append(halve(blocks, bit)[0])
    early = jnp.concatenate(done, axis=0)
    er, late = early.shape[0], CHUNKS[-1]
    part = halve(product(received[-1], amplitudes).reshape(n, late, a), 1)
    row_part = part.reshape(chips, late, chips, width).transpose(0, 2, 1, 3).reshape(chips, -1, width)
    col_part = part.reshape(chips * late, chips, width).transpose(1, 0, 2)
    early_part = early.reshape(er, chips, width).transpose(1, 0, 2)
    got = exchange(jnp.concatenate([row_part, col_part, early_part], axis=1), same_core)
    split = chips * late
    sums = got[:, : 2 * split].sum(0)
    late_rows = sums[:split].reshape(chips, late, width).transpose(1, 0, 2).reshape(late, a)
    late_cols = sums[split:].reshape(chips, late, width)
    cols = jnp.concatenate([got[:, 2 * split :], late_cols], axis=1)
    other = lax.ppermute(cols, AXIS, [(i, i ^ 1) for i in range(n)])
    stacked = jnp.where(core == 0, jnp.stack([cols, other], 1), jnp.stack([other, cols], 1))
    stacked = stacked.reshape(n * rows, 2, width // 2)
    swapped = jnp.where(core == 0, stacked[:, 0], stacked[:, 1])
    paired = jnp.concatenate([early, late_rows], axis=0) + swapped.T
    return paired[:, None, :] / denominator(pair_energy, vir_energy, me * rows, rows)


def solution(mesh):
    n = mesh.shape[AXIS]
    body = exchanged_body if 2 <= n <= 16 and n & (n - 1) == 0 else gathered_body
    in_specs = (P(("grp", AXIS), None, None), P("grp", None, AXIS, None), P("grp"), P("grp"))
    out_specs = P(("grp", AXIS), None, None)
    return jax.shard_map(body, mesh=mesh, in_specs=in_specs, out_specs=out_specs, check_vma=False)
```

```python
import functools
import jax
import jax.numpy as jnp
from jax import lax
from jax.experimental import pallas as pl
from jax.experimental.pallas import tpu as pltpu
from jax.sharding import PartitionSpec as P

AXIS = "vir"
CHUNKS = (8, 32, 16, 8)
STEPS = (2, 1)
SUBLANES = 8


def denominator(pair_energy, vir_energy, start, rows):
    mine = lax.dynamic_slice_in_dim(vir_energy, start, rows, 0)
    return pair_energy[None, :, None] - vir_energy[None, None, :] - mine[:, None, None]


def gathered_body(amplitudes, integrals, pair_energy, vir_energy):
    blocks = lax.all_to_all(integrals, AXIS, split_axis=1, concat_axis=2, tiled=True)
    rows = blocks.shape[2] // lax.axis_size(AXIS)
    part = jnp.einsum("lgif,gfh->ilh", blocks, amplitudes, preferred_element_type=jnp.float32)
    cycle = lax.psum_scatter(part, AXIS, scatter_dimension=0, tiled=True)
    swapped = lax.all_to_all(cycle, AXIS, split_axis=2, concat_axis=0, tiled=True)
    paired = cycle + jnp.transpose(swapped, (2, 1, 0))
    return paired / denominator(pair_energy, vir_energy, lax.axis_index(AXIS) * rows, rows)


def exponent_of(largest):
    return jnp.ceil(jnp.log2(jnp.maximum(largest, 2.0**-100))) - 14.0


def after(x, *deps):
    return lax.optimization_barrier((x, *deps))[0] if deps else x


def product_kernel(blocks, amp, out):
    n, owned, r, e = blocks.shape

    def rows_of(m):
        rows = blocks[:, m]
        if r % 16:
            rows = rows.astype(jnp.float32).reshape(n * r, e).astype(jnp.bfloat16)
        return rows.reshape(n * r, e)

    lhs = jnp.concatenate([rows_of(m) for m in range(owned)], axis=1)
    part = jnp.dot(lhs, amp[...].reshape(owned * e, -1), preferred_element_type=jnp.float32)

    @pl.when(pl.program_id(0) == 0)
    def _():
        out[...] = part

    @pl.when(pl.program_id(0) != 0)
    def _():
        out[...] += part


def product(blocks, amplitudes):
    n, own, r, e = blocks.shape
    a = amplitudes.shape[2]
    step = next(s for s in STEPS if own % s == 0)
    return pl.pallas_call(
        product_kernel,
        grid=(own // step,),
        in_specs=[
            pl.BlockSpec((n, step, r, e), lambda m: (0, m, 0, 0)),
            pl.BlockSpec((step, e, a), lambda m: (m, 0, 0)),
        ],
        out_specs=pl.BlockSpec((n * r, a), lambda m: (0, 0)),
        out_shape=jax.ShapeDtypeStruct((n * r, a), jnp.float32),
        compiler_params=pltpu.CompilerParams(vmem_limit_bytes=48 * 1024 * 1024),
        cost_estimate=pl.CostEstimate(
            flops=2 * n * r * own * e * a,
            bytes_accessed=2 * own * e * (a + n * r) + 4 * n * r * a,
            transcendentals=0,
        ),
    )(blocks, amplitudes)


def exchanged_body(amplitudes, integrals, pair_energy, vir_energy):
    n = lax.axis_size(AXIS)
    chips = n // 2
    me = lax.axis_index(AXIS)
    core = me % 2
    own, e, a = amplitudes.shape
    rows = integrals.shape[2]
    source = integrals.reshape(n, own, rows, e)
    width = a // chips
    same_core = [list(range(c, n, 2)) for c in range(2)]
    starts = [sum(CHUNKS[:q]) for q in range(len(CHUNKS))]

    def exchange(x, groups=None):
        return lax.all_to_all(
            x, AXIS, split_axis=0, concat_axis=0, tiled=True, axis_index_groups=groups
        )

    def halve(blocks, bit):
        odd = (me & bit) != 0
        pair = blocks.reshape(-1, 2, *blocks.shape[1:])
        mine = jnp.where(odd, pair[:, 1], pair[:, 0])
        other = jnp.where(odd, pair[:, 0], pair[:, 1])
        return mine + lax.ppermute(other, AXIS, [(i, i ^ bit) for i in range(n)])

    received, near, done = [], [], []
    for q, r in enumerate(CHUNKS):
        x = source
        if q >= 2:
            x = after(x, received[q - 2])
        x = x[:, :, starts[q] : starts[q] + r]
        if q >= 1:
            x = after(x, received[q - 1], *done[q - 2 : q - 1] if q >= 2 else ())
        received.append(exchange(x))
        if q >= 1:
            blocks = product(received[q - 1], amplitudes).reshape(n, CHUNKS[q - 1], a)
            bit = 1
            while 2 * bit < n:
                blocks = halve(blocks, bit)
                bit *= 2
            near.append(blocks)
            done.append(halve(blocks, bit)[0])
    early = jnp.concatenate(done, axis=0)
    er, late = early.shape[0], CHUNKS[-1]
    part = halve(product(received[-1], amplitudes).reshape(n, late, a), 1)
    row_part = part.reshape(chips, late, chips, width).transpose(0, 2, 1, 3).reshape(chips, -1, width)
    col_part = part.reshape(chips * late, chips, width).transpose(1, 0, 2)
    early_part = early.reshape(er, chips, width).transpose(1, 0, 2)
    exponent = exponent_of(jnp.maximum(jnp.max(jnp.abs(part)), jnp.max(jnp.abs(early))))
    parts = jnp.concatenate([row_part, col_part, early_part], axis=1) * jnp.exp2(-exponent)
    tag = jnp.full((chips, SUBLANES, width), exponent, jnp.float32)
    sent = jnp.concatenate([parts, tag], axis=1).astype(jnp.float16)
    got = exchange(sent, same_core).astype(jnp.float32)
    got = got[:, :-SUBLANES] * jnp.exp2(got[:, -1:, :])
    split = chips * late
    sums = got[:, : 2 * split].sum(0)
    late_rows = sums[:split].reshape(chips, late, width).transpose(1, 0, 2).reshape(late, a)
    late_cols = sums[split:].reshape(chips, late, width)
    cols = jnp.concatenate([got[:, 2 * split :], late_cols], axis=1)
    other = lax.ppermute(cols, AXIS, [(i, i ^ 1) for i in range(n)])
    stacked = jnp.where(core == 0, jnp.stack([cols, other], 1), jnp.stack([other, cols], 1))
    stacked = stacked.reshape(n * rows, 2, width // 2)
    swapped = jnp.where(core == 0, stacked[:, 0], stacked[:, 1])
    paired = jnp.concatenate([early, late_rows], axis=0) + swapped.T
    return paired[:, None, :] / denominator(pair_energy, vir_energy, me * rows, rows)


def solution(mesh):
    n = mesh.shape[AXIS]
    body = exchanged_body if 2 <= n <= 16 and n & (n - 1) == 0 else gathered_body
    in_specs = (P(("grp", AXIS), None, None), P("grp", None, AXIS, None), P("grp"), P("grp"))
    out_specs = P(("grp", AXIS), None, None)
    return jax.shard_map(body, mesh=mesh, in_specs=in_specs, out_specs=out_specs, check_vma=False)
```

```python
import functools
import jax
import jax.numpy as jnp
from jax import lax
from jax.experimental import pallas as pl
from jax.experimental.pallas import tpu as pltpu
from jax.sharding import PartitionSpec as P

AXIS = "vir"
CHUNKS = (24, 32, 8)
STEPS = (2, 1)
SUBLANES = 8


def denominator(pair_energy, vir_energy, start, rows):
    mine = lax.dynamic_slice_in_dim(vir_energy, start, rows, 0)
    return pair_energy[None, :, None] - vir_energy[None, None, :] - mine[:, None, None]


def gathered_body(amplitudes, integrals, pair_energy, vir_energy):
    blocks = lax.all_to_all(integrals, AXIS, split_axis=1, concat_axis=2, tiled=True)
    rows = blocks.shape[2] // lax.axis_size(AXIS)
    part = jnp.einsum("lgif,gfh->ilh", blocks, amplitudes, preferred_element_type=jnp.float32)
    cycle = lax.psum_scatter(part, AXIS, scatter_dimension=0, tiled=True)
    swapped = lax.all_to_all(cycle, AXIS, split_axis=2, concat_axis=0, tiled=True)
    paired = cycle + jnp.transpose(swapped, (2, 1, 0))
    return paired / denominator(pair_energy, vir_energy, lax.axis_index(AXIS) * rows, rows)


def exponent_of(largest):
    return jnp.ceil(jnp.log2(jnp.maximum(largest, 2.0**-100))) - 14.0


def after(x, *deps):
    return lax.optimization_barrier((x, *deps))[0] if deps else x


def product_kernel(blocks, amp, out):
    n, owned, r, e = blocks.shape

    def rows_of(m):
        rows = blocks[:, m]
        if r % 16:
            rows = rows.astype(jnp.float32).reshape(n * r, e).astype(jnp.bfloat16)
        return rows.reshape(n * r, e)

    lhs = jnp.concatenate([rows_of(m) for m in range(owned)], axis=1)
    part = jnp.dot(lhs, amp[...].reshape(owned * e, -1), preferred_element_type=jnp.float32)

    @pl.when(pl.program_id(0) == 0)
    def _():
        out[...] = part

    @pl.when(pl.program_id(0) != 0)
    def _():
        out[...] += part


def product(blocks, amplitudes):
    n, own, r, e = blocks.shape
    a = amplitudes.shape[2]
    step = next(s for s in STEPS if own % s == 0)
    return pl.pallas_call(
        product_kernel,
        grid=(own // step,),
        in_specs=[
            pl.BlockSpec((n, step, r, e), lambda m: (0, m, 0, 0)),
            pl.BlockSpec((step, e, a), lambda m: (m, 0, 0)),
        ],
        out_specs=pl.BlockSpec((n * r, a), lambda m: (0, 0)),
        out_shape=jax.ShapeDtypeStruct((n * r, a), jnp.float32),
        compiler_params=pltpu.CompilerParams(vmem_limit_bytes=48 * 1024 * 1024),
        cost_estimate=pl.CostEstimate(
            flops=2 * n * r * own * e * a,
            bytes_accessed=2 * own * e * (a + n * r) + 4 * n * r * a,
            transcendentals=0,
        ),
    )(blocks, amplitudes)


def combine_kernel(core, cols, other, mine, base, energy, out):
    first = core[0] == 0
    half = cols.shape[2] // 2
    for k in range(cols.shape[0]):
        even = jnp.where(first, cols[k], other[k])
        odd = jnp.where(first, other[k], cols[k])
        both = jnp.concatenate([even, odd], axis=0)
        block = jnp.where(first, both[:, :half], both[:, half:]).T
        at = pl.ds(k * block.shape[1], block.shape[1])
        out[:, 0, at] = (mine[:, at] + block) / (base[...] - energy[:, at])


def combined(core, cols, other, mine, base, energy):
    rows, a = mine.shape
    return pl.pallas_call(
        combine_kernel,
        in_specs=[pl.BlockSpec(memory_space=pltpu.SMEM)]
        + [pl.BlockSpec(memory_space=pltpu.VMEM)] * 5,
        out_specs=pl.BlockSpec(memory_space=pltpu.VMEM),
        out_shape=jax.ShapeDtypeStruct((rows, 1, a), jnp.float32),
        compiler_params=pltpu.CompilerParams(vmem_limit_bytes=16 * 1024 * 1024),
    )(core, cols, other, mine, base, energy)


def exchanged_body(amplitudes, integrals, pair_energy, vir_energy):
    n = lax.axis_size(AXIS)
    chips = n // 2
    me = lax.axis_index(AXIS)
    core = me % 2
    own, e, a = amplitudes.shape
    rows = integrals.shape[2]
    source = integrals.reshape(n, own, rows, e)
    width = a // chips
    same_core = [list(range(c, n, 2)) for c in range(2)]
    starts = [sum(CHUNKS[:q]) for q in range(len(CHUNKS))]

    def exchange(x, groups=None):
        return lax.all_to_all(
            x, AXIS, split_axis=0, concat_axis=0, tiled=True, axis_index_groups=groups
        )

    def halve(blocks, bit):
        odd = (me & bit) != 0
        pair = blocks.reshape(-1, 2, *blocks.shape[1:])
        mine = jnp.where(odd, pair[:, 1], pair[:, 0])
        other = jnp.where(odd, pair[:, 0], pair[:, 1])
        return mine + lax.ppermute(other, AXIS, [(i, i ^ bit) for i in range(n)])

    received, near, done = [], [], []
    for q, r in enumerate(CHUNKS):
        x = source
        if q >= 2:
            x = after(x, received[q - 2])
        x = x[:, :, starts[q] : starts[q] + r]
        if q >= 1:
            x = after(x, received[q - 1], *done[q - 2 : q - 1] if q >= 2 else ())
        received.append(exchange(x))
        if q >= 1:
            blocks = product(received[q - 1], amplitudes).reshape(n, CHUNKS[q - 1], a)
            bit = 1
            while 2 * bit < n:
                blocks = halve(blocks, bit)
                bit *= 2
            near.append(blocks)
            if q == len(CHUNKS) - 1:
                blocks = after(blocks, received[q])
            done.append(halve(blocks, bit)[0])
    early = jnp.concatenate(done, axis=0)
    er, late = early.shape[0], CHUNKS[-1]
    part = halve(product(received[-1], amplitudes).reshape(n, late, a), 1)
    row_part = part.reshape(chips, late, chips, width).transpose(0, 2, 1, 3).reshape(chips, -1, width)
    col_part = part.reshape(chips * late, chips, width).transpose(1, 0, 2)
    early_part = early.reshape(er, chips, width).transpose(1, 0, 2)
    parts = jnp.concatenate([row_part, col_part, early_part], axis=1)
    exponent = exponent_of(jnp.max(jnp.abs(parts), axis=(0, 1), keepdims=True))
    tag = jnp.broadcast_to(exponent, (chips, SUBLANES, width))
    sent = jnp.concatenate([parts * jnp.exp2(-exponent), tag], axis=1).astype(jnp.float16)
    got = exchange(sent, same_core).astype(jnp.float32)
    got = got[:, :-SUBLANES] * jnp.exp2(got[:, -1:, :])
    split = chips * late
    sums = got[:, : 2 * split].sum(0)
    late_rows = sums[:split].reshape(chips, late, width).transpose(1, 0, 2).reshape(late, a)
    late_cols = sums[split:].reshape(chips, late, width)
    cols = jnp.concatenate([got[:, 2 * split :], late_cols], axis=1)
    other = lax.ppermute(cols, AXIS, [(i, i ^ 1) for i in range(n)])
    mine = jnp.concatenate([early, late_rows], axis=0)
    base = pair_energy - lax.dynamic_slice_in_dim(vir_energy, me * rows, rows, 0)
    return combined(core.reshape(1), cols, other, mine, base[:, None], vir_energy[None, :])


def solution(mesh):
    n = mesh.shape[AXIS]
    body = exchanged_body if 2 <= n <= 16 and n & (n - 1) == 0 else gathered_body
    in_specs = (P(("grp", AXIS), None, None), P("grp", None, AXIS, None), P("grp"), P("grp"))
    out_specs = P(("grp", AXIS), None, None)
    return jax.shard_map(body, mesh=mesh, in_specs=in_specs, out_specs=out_specs, check_vma=False)
```

```python
import functools
import jax
import jax.numpy as jnp
from jax import lax
from jax.experimental import pallas as pl
from jax.experimental.pallas import tpu as pltpu
from jax.sharding import PartitionSpec as P

AXIS = "vir"
CHUNKS = (32, 24, 8)
STEPS = (2, 1)
SUBLANES = 8
PIECES = 16


def denominator(pair_energy, vir_energy, start, rows):
    mine = lax.dynamic_slice_in_dim(vir_energy, start, rows, 0)
    return pair_energy[None, :, None] - vir_energy[None, None, :] - mine[:, None, None]


def gathered_body(amplitudes, integrals, pair_energy, vir_energy):
    blocks = lax.all_to_all(integrals, AXIS, split_axis=1, concat_axis=2, tiled=True)
    rows = blocks.shape[2] // lax.axis_size(AXIS)
    part = jnp.einsum("lgif,gfh->ilh", blocks, amplitudes, preferred_element_type=jnp.float32)
    cycle = lax.psum_scatter(part, AXIS, scatter_dimension=0, tiled=True)
    swapped = lax.all_to_all(cycle, AXIS, split_axis=2, concat_axis=0, tiled=True)
    paired = cycle + jnp.transpose(swapped, (2, 1, 0))
    return paired / denominator(pair_energy, vir_energy, lax.axis_index(AXIS) * rows, rows)


def exponent_of(largest):
    return jnp.ceil(jnp.log2(jnp.maximum(largest, 2.0**-100))) - 14.0


def after(x, *deps):
    return lax.optimization_barrier((x, *deps))[0] if deps else x


def head_kernel(source, out, held, load_sem, store_sem):
    m, r, _ = held.shape
    size = m // load_sem.shape[0]
    stores = []
    loads = []
    for k in range(load_sem.shape[0]):
        at = pl.ds(k * size, size)
        loads.append(
            pltpu.make_async_copy(source.at[at, pl.ds(0, r)], held.at[at], load_sem.at[k])
        )
        stores.append(pltpu.make_async_copy(held.at[at], out.at[at], store_sem.at[k]))
    for load in loads:
        load.start()
    for load, store in zip(loads, stores):
        load.wait()
        store.start()
    for store in stores:
        store.wait()


def head(source, r):
    m, _, e = source.shape
    shape = (m, r, e)
    pieces = next(k for k in (PIECES, 8, 4, 2, 1) if m % k == 0)
    return pl.pallas_call(
        head_kernel,
        in_specs=[pl.BlockSpec(memory_space=pl.ANY)],
        out_specs=pl.BlockSpec(memory_space=pl.ANY),
        out_shape=jax.ShapeDtypeStruct(shape, source.dtype),
        scratch_shapes=[
            pltpu.VMEM(shape, source.dtype),
            pltpu.SemaphoreType.DMA((pieces,)),
            pltpu.SemaphoreType.DMA((pieces,)),
        ],
        compiler_params=pltpu.CompilerParams(vmem_limit_bytes=60 * 1024 * 1024),
        cost_estimate=pl.CostEstimate(
            flops=0, bytes_accessed=4 * m * r * e, transcendentals=0
        ),
    )(source)


def product_kernel(blocks, amp, out):
    n, owned, r, e = blocks.shape

    def rows_of(m):
        rows = blocks[:, m]
        if r % 16:
            rows = rows.astype(jnp.float32).reshape(n * r, e).astype(jnp.bfloat16)
        return rows.reshape(n * r, e)

    lhs = jnp.concatenate([rows_of(m) for m in range(owned)], axis=1)
    part = jnp.dot(lhs, amp[...].reshape(owned * e, -1), preferred_element_type=jnp.float32)

    @pl.when(pl.program_id(0) == 0)
    def _():
        out[...] = part

    @pl.when(pl.program_id(0) != 0)
    def _():
        out[...] += part


def product(blocks, amplitudes):
    n, own, r, e = blocks.shape
    a = amplitudes.shape[2]
    step = next(s for s in STEPS if own % s == 0)
    return pl.pallas_call(
        product_kernel,
        grid=(own // step,),
        in_specs=[
            pl.BlockSpec((n, step, r, e), lambda m: (0, m, 0, 0)),
            pl.BlockSpec((step, e, a), lambda m: (m, 0, 0)),
        ],
        out_specs=pl.BlockSpec((n * r, a), lambda m: (0, 0)),
        out_shape=jax.ShapeDtypeStruct((n * r, a), jnp.float32),
        compiler_params=pltpu.CompilerParams(vmem_limit_bytes=48 * 1024 * 1024),
        cost_estimate=pl.CostEstimate(
            flops=2 * n * r * own * e * a,
            bytes_accessed=2 * own * e * (a + n * r) + 4 * n * r * a,
            transcendentals=0,
        ),
    )(blocks, amplitudes)


def combine_kernel(core, cols, other, mine, base, energy, out):
    first = core[0] == 0
    half = cols.shape[2] // 2
    for k in range(cols.shape[0]):
        even = jnp.where(first, cols[k], other[k])
        odd = jnp.where(first, other[k], cols[k])
        both = jnp.concatenate([even, odd], axis=0)
        block = jnp.where(first, both[:, :half], both[:, half:]).T
        at = pl.ds(k * block.shape[1], block.shape[1])
        out[:, 0, at] = (mine[:, at] + block) / (base[...] - energy[:, at])


def combined(core, cols, other, mine, base, energy):
    rows, a = mine.shape
    return pl.pallas_call(
        combine_kernel,
        in_specs=[pl.BlockSpec(memory_space=pltpu.SMEM)]
        + [pl.BlockSpec(memory_space=pltpu.VMEM)] * 5,
        out_specs=pl.BlockSpec(memory_space=pltpu.VMEM),
        out_shape=jax.ShapeDtypeStruct((rows, 1, a), jnp.float32),
        compiler_params=pltpu.CompilerParams(vmem_limit_bytes=16 * 1024 * 1024),
    )(core, cols, other, mine, base, energy)


def exchanged_body(amplitudes, integrals, pair_energy, vir_energy):
    n = lax.axis_size(AXIS)
    chips = n // 2
    me = lax.axis_index(AXIS)
    core = me % 2
    own, e, a = amplitudes.shape
    rows = integrals.shape[2]
    source = integrals.reshape(n, own, rows, e)
    width = a // chips
    same_core = [list(range(c, n, 2)) for c in range(2)]
    starts = [sum(CHUNKS[:q]) for q in range(len(CHUNKS))]

    def exchange(x, groups=None):
        return lax.all_to_all(
            x, AXIS, split_axis=0, concat_axis=0, tiled=True, axis_index_groups=groups
        )

    def halve(blocks, bit):
        odd = (me & bit) != 0
        pair = blocks.reshape(-1, 2, *blocks.shape[1:])
        mine = jnp.where(odd, pair[:, 1], pair[:, 0])
        other = jnp.where(odd, pair[:, 0], pair[:, 1])
        return mine + lax.ppermute(other, AXIS, [(i, i ^ bit) for i in range(n)])

    received, near = [], []
    for q, r in enumerate(CHUNKS):
        x = source
        if q >= 2:
            x = after(x, received[q - 2])
        if q == 0 and r % 16 == 0:
            x = head(x.reshape(n * own, rows, e), r).reshape(n, own, r, e)
        else:
            x = x[:, :, starts[q] : starts[q] + r]
        if q >= 1:
            x = after(x, received[q - 1], *near[q - 2 : q - 1] if q >= 2 else ())
        received.append(exchange(x))
        if q >= 1:
            blocks = product(received[q - 1], amplitudes).reshape(n, CHUNKS[q - 1], a)
            bit = 1
            while 2 * bit < n:
                blocks = halve(blocks, bit)
                bit *= 2
            near.append(blocks)
    split = jnp.concatenate(near, axis=1)
    early = halve(after(split, received[-1]), chips)[0]
    er, late = early.shape[0], CHUNKS[-1]
    part = halve(product(received[-1], amplitudes).reshape(n, late, a), 1)
    row_part = part.reshape(chips, late, chips, width).transpose(0, 2, 1, 3).reshape(chips, -1, width)
    col_part = part.reshape(chips * late, chips, width).transpose(1, 0, 2)
    early_part = early.reshape(er, chips, width).transpose(1, 0, 2)
    parts = jnp.concatenate([row_part, col_part, early_part], axis=1)
    exponent = exponent_of(jnp.max(jnp.abs(parts), axis=(0, 1), keepdims=True))
    tag = jnp.broadcast_to(exponent, (chips, SUBLANES, width))
    sent = jnp.concatenate([parts * jnp.exp2(-exponent), tag], axis=1).astype(jnp.float16)
    got = exchange(sent, same_core).astype(jnp.float32)
    got = got[:, :-SUBLANES] * jnp.exp2(got[:, -1:, :])
    split = chips * late
    sums = got[:, : 2 * split].sum(0)
    late_rows = sums[:split].reshape(chips, late, width).transpose(1, 0, 2).reshape(late, a)
    late_cols = sums[split:].reshape(chips, late, width)
    cols = jnp.concatenate([got[:, 2 * split :], late_cols], axis=1)
    other = lax.ppermute(cols, AXIS, [(i, i ^ 1) for i in range(n)])
    mine = jnp.concatenate([early, late_rows], axis=0)
    base = pair_energy - lax.dynamic_slice_in_dim(vir_energy, me * rows, rows, 0)
    return combined(core.reshape(1), cols, other, mine, base[:, None], vir_energy[None, :])


def solution(mesh):
    n = mesh.shape[AXIS]
    body = exchanged_body if 2 <= n <= 16 and n & (n - 1) == 0 else gathered_body
    in_specs = (P(("grp", AXIS), None, None), P("grp", None, AXIS, None), P("grp"), P("grp"))
    out_specs = P(("grp", AXIS), None, None)
    return jax.shard_map(body, mesh=mesh, in_specs=in_specs, out_specs=out_specs, check_vma=False)
```
